256 devices in a mesh: tp: 16 (over z, x_hi), fsdp: 16 (over y, x_lo, core).
Axes of the slice: x: 4 (x_hi: 2, x_lo: 2; x = x_hi * 2 + x_lo), y: 4, z: 8, core: 2. Of those that a mesh axis runs over, the one named last changes fastest.
Arguments:
- activations: bfloat16 [16, 1024, 8192], P('fsdp', 'tp'), may hold values from -6 to 6
- grad_output: bfloat16 [16, 1024, 28672], P('fsdp', None, 'tp'), may hold values from -0.01171875 to 0.01171875
- projection: bfloat16 [8192, 512], P('fsdp'), may hold values from -0.25 to 0.25
- piece_lengths: int32 [16], replicated, may hold values from 1 to 48, 512 in all
- piece_owners: int32 [16], replicated, may hold values from 0 to 15, as said below
- first_moment: float32 [768, 28672], P('fsdp', 'tp'), may hold values from -3 to 3
- second_moment: float32 [768, 28672], P('fsdp', 'tp'), may hold values from 0.0005 to 0.005
Outputs:
- weight_delta: bfloat16 [8192, 28672], P('fsdp', 'tp')
- new_first: float32 [768, 28672], P('fsdp', 'tp')
- new_second: float32 [768, 28672], P('fsdp', 'tp')
The draws below stay inside these ranges and needn't reach their ends.
Inputs may be any that keep to these rules, and one draw needn't show every extreme that they name: `piece_lengths`: the lengths sum to 512; one of them is exactly 48. `piece_owners`: each owner appears exactly once.
All inputs are finite; a program needn't handle non-finite values.
Results may differ from the reference program's by a relative error of at most 0.0052.
Values may be sent and summed in bfloat16 or wider, within the bound.
No kernel may reach another device: no remote copies, remote signals or barrier semaphores. Data moves between devices by JAX's collectives and lax.ppermute only.
A program may use at most 128 MiB of HBM per device.

```python
import math
import jax
import jax.numpy as jnp
import numpy as np
from jax import lax

D = 8192
FF = 28672
RANK = 512
STEP = 10
MICRO = 1024
MOST = 48
N_FSDP = 16


def draw_piece_owners(key, part):
    key = jax.random.fold_in(key, 7919)
    return jax.random.permutation(key, jnp.arange(N_FSDP, dtype=jnp.int32)).astype(jnp.int32)


def block_scale(key, dims, cuts, least, high):
    def one(dim, parts):
        steps = jax.random.uniform(jax.random.fold_in(jax.random.fold_in(key, 6), dim), (parts,), jnp.float32, least / len(cuts), high / len(cuts))
        return jnp.repeat(jnp.exp(steps), dims[dim] // parts).reshape((-1,) + (1,) * (len(dims) - dim - 1))

    loudness = one(*cuts[0])
    for cut in cuts[1:]:
        loudness = loudness * one(*cut)
    return loudness


def length_profile(number_of, total, limit, skew):
    loads = [(1 << 20) // math.isqrt(standing ** skew) + 1 for standing in range(2, number_of + 1)]
    spare, holding = total - limit - (number_of - 1), [1] * (number_of - 1)
    while spare > 0:
        candidates = [i for i in range(number_of - 1) if holding[i] < limit]
        whole, remaining = sum([loads[i] for i in candidates]), spare
        for i in candidates:
            addition = min(limit - holding[i], max(1, remaining * loads[i] // whole), spare)
            holding[i] = holding[i] + addition
            spare = spare - addition
    return np.array([limit] + holding)


def uneven(key, amount, total, most, lean):
    if amount == 2:
        one = jax.random.randint(key, (), max(1, total - most), min(most, total - 1) + 1)
        return jnp.stack([one, total - one])
    sizes = jnp.asarray(length_profile(amount, total, most, lean), jnp.int32)
    pairs = (amount - 1) // 2
    giver, receiver = sizes[1:1 + 2 * pairs:2], sizes[2:2 + 2 * pairs:2]
    slack = jnp.minimum(giver - 1, most - receiver)
    moved = jax.random.randint(jax.random.fold_in(key, 1), (pairs,), 0, 1 << 20) % (slack + 1)
    sizes = sizes.at[1:1 + 2 * pairs:2].set(giver - moved).at[2:2 + 2 * pairs:2].set(receiver + moved)
    return sizes[jax.random.permutation(jax.random.fold_in(key, 2), amount)]


def gaussian(rng, shape, scale, most, shards=(), kind=jnp.bfloat16):
    level = block_scale(rng, shape, shards, -0.22, 0.18) if shards else 1.0
    values = jax.random.normal(rng, shape, jnp.float32) * scale * level
    return jnp.minimum(jnp.maximum(values, -most), most).astype(kind)


def setup_inputs(seed: int = 0) -> dict:
    seeds = jax.random.split(jax.random.key(seed), 8)
    activations = gaussian(seeds[0], (N_FSDP, MICRO, D), 1.0, 6.0, ((0, 16), (1, 16)))
    grad_output = gaussian(seeds[1], (N_FSDP, MICRO, FF), (N_FSDP * MICRO * D // RANK) ** -0.5, 0.01171875, ((0, 16), (2, 16)))
    projection = gaussian(seeds[2], (D, RANK), RANK ** -0.5, 0.25, ((0, 16),))
    piece_lengths = uneven(seeds[3], N_FSDP, RANK, MOST, 2).astype(jnp.int32)
    piece_owners = draw_piece_owners(jax.random.fold_in(seeds[7], 71), 0)
    first_moment = gaussian(seeds[5], (N_FSDP * MOST, FF), 0.2, 3.0, ((0, 16), (1, 16)), jnp.float32)
    second_moment = jnp.clip(jnp.exp(math.log(0.005) - 2.30258502 * jax.random.uniform(seeds[6], (N_FSDP * MOST, FF), jnp.float32) ** block_scale(seeds[6], (N_FSDP * MOST, FF), ((0, 16), (1, 16)), -0.2, 0.2)), 0.0005, 0.005)
    return {"activations": activations, "grad_output": grad_output, "projection": projection, "piece_lengths": piece_lengths, "piece_owners": piece_owners, "first_moment": first_moment, "second_moment": second_moment}


beta_one = 0.9
beta_two = 0.999
adam_eps = 1e-08

def slot_table(piece_lengths, piece_owners, owner_count, slot_count):
    owner_order = jnp.arange(owner_count, dtype=jnp.int32)
    piece_starts = (jnp.cumsum(piece_lengths) - piece_lengths).astype(jnp.int32)
    matches = (piece_owners[None, :] == owner_order[:, None]).astype(jnp.int32)
    own_start = lax.optimization_barrier(jnp.sum(matches * piece_starts[None, :], axis=1)).astype(jnp.int32)
    own_length = lax.optimization_barrier(jnp.sum(matches * piece_lengths[None, :], axis=1)).astype(jnp.int32)
    slot_offsets = jnp.arange(slot_count, dtype=jnp.int32)
    rank_rows = own_start[:, None] + slot_offsets[None, :]
    live_rows = slot_offsets[None, :] < own_length[:, None]
    return (rank_rows.reshape(-1).astype(jnp.int32), live_rows.reshape(-1))

def adam_rows(gradient, live_rows, first_moment, second_moment):
    live_mask = live_rows[:, None]
    new_first = jnp.where(live_mask, beta_one * first_moment + (1.0 - beta_one) * gradient, 0.0)
    new_second = jnp.where(live_mask, beta_two * second_moment + (1.0 - beta_two) * gradient * gradient, 0.0)
    first_hat = new_first / (1.0 - beta_one ** STEP)
    second_hat = new_second / (1.0 - beta_two ** STEP)
    update = jnp.where(live_mask, first_hat / (jnp.sqrt(second_hat) + adam_eps), 0.0)
    return (new_first, new_second, update.astype(jnp.bfloat16))

def reference(activations, grad_output, projection, piece_lengths, piece_owners, first_moment, second_moment):
    tokens_all = activations.reshape(-1, D)
    projected = jnp.dot(tokens_all, projection, preferred_element_type=jnp.float32).astype(jnp.bfloat16)
    outputs_all = grad_output.reshape(-1, FF)
    gradient = lax.dot_general(projected, outputs_all, (((0,), (0,)), ((), ())), preferred_element_type=jnp.float32)
    rank_rows, live_rows = slot_table(piece_lengths, piece_owners, N_FSDP, MOST)
    safe_rows = jnp.clip(rank_rows, 0, RANK - 1)
    picked = jnp.take(gradient, safe_rows, axis=0)
    new_first, new_second, update = adam_rows(picked, live_rows, first_moment, second_moment)
    placement = ((rank_rows[None, :] == jnp.arange(RANK, dtype=jnp.int32)[:, None]) & live_rows[None, :]).astype(jnp.bfloat16)
    full_update = jnp.dot(placement, update, preferred_element_type=jnp.float32).astype(jnp.bfloat16)
    weight_delta = jnp.dot(projection, full_update, preferred_element_type=jnp.float32).astype(jnp.bfloat16)
    return (weight_delta, new_first, new_second)
```

```python
import functools

import jax
import jax.numpy as jnp
from jax import lax
from jax.experimental import pallas as pl
from jax.experimental.pallas import tpu as pltpu
from jax.sharding import PartitionSpec as P

STEP = 10
beta_one = 0.9
beta_two = 0.999
adam_eps = 1e-08

F32 = jnp.float32
BF16 = jnp.bfloat16

CHIPS = [(dy, dx) for dy in range(4) for dx in range(2)]


def fsdp_shift(value, dy, dx, dk):
    pairs = [
        (i, ((i // 4 + dy) % 4) * 4 + ((i // 2 % 2) ^ dx) * 2 + ((i % 2) ^ dk)) for i in range(16)
    ]
    return lax.ppermute(value, "fsdp", pairs)


def tp_shift(value, dz, dh):
    pairs = [(i, ((i // 2 + dz) % 8) * 2 + ((i % 2) ^ dh)) for i in range(16)]
    return lax.ppermute(value, "tp", pairs)


def front_kernel(where_ref, a0, a1, a2, a3, p0, p1, p2, p3, o0, o1, o2, o3):
    low = where_ref[1]
    total = None
    for r, p in enumerate((p0, p1, p2, p3)):
        columns = pl.ds(pl.multiple_of((low ^ r) * 512, 512), 512)
        rows = jnp.concatenate([a[:, columns] for a in (a0, a1, a2, a3)], axis=0)
        term = jnp.dot(rows, p[...], preferred_element_type=F32)
        total = term if total is None else total + term
    for s, o in enumerate((o0, o1, o2, o3)):
        o[...] = total[s * 64 : (s + 1) * 64].astype(o.dtype)


def front(where, tokens, received, blocks):
    whole = lambda shape: pl.BlockSpec(shape, lambda i, w: (0, 0))
    return pl.pallas_call(
        front_kernel,
        grid_spec=pltpu.PrefetchScalarGridSpec(
            num_scalar_prefetch=1,
            grid=(1,),
            in_specs=[pl.BlockSpec((64, 2048), lambda i, w: (0, w[0]))]
            + [whole((64, 2048))] * 3
            + [whole((512, 512))] * 4,
            out_specs=[whole((64, 512))] * 4,
        ),
        out_shape=[jax.ShapeDtypeStruct((64, 512), F32)] * 4,
        cost_estimate=pl.CostEstimate(flops=2 * 256 * 2048 * 512, bytes_accessed=3 << 20, transcendentals=0),
        name="front",
    )(where, tokens, *received, *blocks)


def gradient_kernel(where_ref, b0, b1, b2, b3, b4, b5, b6, b7, select, grads, out, left):
    @pl.when(pl.program_id(0) == 0)
    def _():
        z = where_ref[2]
        for d, b in enumerate((b0, b1, b2, b3, b4, b5, b6, b7)):
            place = pl.ds(pl.multiple_of(lax.rem(z + 8 - d, 8) * 128, 128), 128)
            left[:, place] = lax.dot_general(
                select[...], b[...], (((1,), (1,)), ((), ())), preferred_element_type=F32
            ).astype(BF16)

    out[...] = jnp.dot(left[...], grads[...], preferred_element_type=F32).astype(out.dtype)


def gradient_rows(where, blocks, select, grads, dtype, name):
    rows = select.shape[0]
    width = 256
    whole = lambda shape: pl.BlockSpec(shape, lambda i, w: (0, 0))
    return pl.pallas_call(
        gradient_kernel,
        grid_spec=pltpu.PrefetchScalarGridSpec(
            num_scalar_prefetch=1,
            grid=(1792 // width,),
            in_specs=[whole((128, 512))] * 8
            + [whole((rows, 512)), pl.BlockSpec((1024, width), lambda i, w: (0, i))],
            out_specs=pl.BlockSpec((rows, width), lambda i, w: (0, i)),
            scratch_shapes=[pltpu.VMEM((rows, 1024), BF16)],
        ),
        out_shape=jax.ShapeDtypeStruct((rows, 1792), dtype),
        cost_estimate=pl.CostEstimate(
            flops=2 * rows * 1024 * 1792, bytes_accessed=6 << 20, transcendentals=0
        ),
        name=name,
    )(where, *blocks, select, grads)


def slots_of(owners, piece_lengths, piece_owners):
    starts = jnp.cumsum(piece_lengths) - piece_lengths
    matches = (piece_owners[None, :] == owners[:, None]).astype(jnp.int32)
    own_start = jnp.sum(matches * starts[None, :], axis=1)
    own_length = jnp.sum(matches * piece_lengths[None, :], axis=1)
    offsets = jnp.arange(48, dtype=jnp.int32)
    rows = own_start[:, None] + offsets[None, :]
    live = offsets[None, :] < own_length[:, None]
    return jnp.where(live, rows, -1).reshape(-1)


def one_hot(rows):
    return (rows[:, None] == jnp.arange(512, dtype=jnp.int32)[None, :]).astype(BF16)


def adam_rows(gradient, live_rows, first_moment, second_moment):
    live_mask = live_rows[:, None]
    new_first = jnp.where(live_mask, beta_one * first_moment + (1.0 - beta_one) * gradient, 0.0)
    new_second = jnp.where(
        live_mask, beta_two * second_moment + (1.0 - beta_two) * gradient * gradient, 0.0
    )
    first_hat = new_first / (1.0 - beta_one**STEP)
    second_hat = new_second / (1.0 - beta_two**STEP)
    update = jnp.where(live_mask, first_hat / (jnp.sqrt(second_hat) + adam_eps), 0.0)
    return (new_first, new_second, update.astype(BF16))


def per_device(
    activations, grad_output, projection, piece_lengths, piece_owners, first_moment, second_moment
):
    tokens = activations[0]
    grads = grad_output[0]
    f = lax.axis_index("fsdp").astype(jnp.int32)
    c = lax.axis_index("tp").astype(jnp.int32)
    y, x, core = f // 4, f // 2 % 2, f % 2
    z, h = c // 2, c % 2
    where = jnp.stack([y, f % 4, z])

    received = [
        fsdp_shift(lax.dynamic_slice(tokens, (0, (y + s) % 4 * 2048), (64, 2048)), s, 0, 0)
        for s in (1, 2, 3)
    ]
    over_x = fsdp_shift(projection, 0, 1, 0)
    over_core = fsdp_shift(projection, 0, 0, 1)
    over_both = fsdp_shift(over_x, 0, 0, 1)
    partial = front(where, tokens, received, (projection, over_core, over_x, over_both))
    total = partial[0]
    for s in (1, 2, 3):
        total = total + fsdp_shift(partial[s], -s, 0, 0)
    projected = total.astype(BF16)

    partner = tp_shift(projected, 0, 1)
    block = jnp.where(
        h == 0,
        jnp.concatenate([projected, partner], axis=0),
        jnp.concatenate([partner, projected], axis=0),
    )
    blocks = [block] + [tp_shift(block, d, 0) for d in range(1, 8)]

    ahead = jnp.stack([(y + dy) % 4 * 4 + (x ^ dx) * 2 for dy, dx in CHIPS])
    behind = jnp.stack([(y - dy) % 4 * 4 + (x ^ dx) * 2 for dy, dx in CHIPS])
    other = 1 - core
    keep_rows = slots_of(ahead + core, piece_lengths, piece_owners)
    give_rows = slots_of(ahead + other, piece_lengths, piece_owners)
    give = gradient_rows(where, blocks, one_hot(give_rows), grads, BF16, "give")
    keep = gradient_rows(where, blocks, one_hot(keep_rows), grads, F32, "keep")
    pair = keep + fsdp_shift(give, 0, 0, 1).astype(F32)
    picked = pair[:48]
    for i, (dy, dx) in enumerate(CHIPS):
        if i:
            piece = pair[48 * i : 48 * i + 48].astype(BF16)
            picked = picked + fsdp_shift(piece, dy, dx, 0).astype(F32)

    new_first, new_second, update = adam_rows(
        picked, keep_rows[:48] >= 0, first_moment, second_moment
    )

    same = one_hot(slots_of(behind + core, piece_lengths, piece_owners))
    cross = one_hot(slots_of(behind + other, piece_lengths, piece_owners))
    over = (((1,), (1,)), ((), ()))
    chosen_same = lax.dot_general(projection, same, over, preferred_element_type=F32).astype(BF16)
    chosen_cross = lax.dot_general(projection, cross, over, preferred_element_type=F32).astype(BF16)
    updates = jnp.concatenate(
        [update] + [fsdp_shift(update, dy, dx, 0) for dy, dx in CHIPS[1:]], axis=0
    )
    crossed = fsdp_shift(updates, 0, 0, 1)
    weight_delta = jnp.dot(chosen_same, updates, preferred_element_type=F32) + jnp.dot(
        chosen_cross, crossed, preferred_element_type=F32
    )
    return (weight_delta.astype(BF16), new_first, new_second)


def solution(mesh):
    return jax.shard_map(
        per_device,
        mesh=mesh,
        in_specs=(
            P("fsdp", "tp", None),
            P("fsdp", None, "tp"),
            P("fsdp", None),
            P(),
            P(),
            P("fsdp", "tp"),
            P("fsdp", "tp"),
        ),
        out_specs=(P("fsdp", "tp"), P("fsdp", "tp"), P("fsdp", "tp")),
        check_vma=False,
    )
```

```python
import functools

import jax
import jax.numpy as jnp
from jax import lax
from jax.experimental import pallas as pl
from jax.experimental.pallas import tpu as pltpu
from jax.sharding import PartitionSpec as P

STEP = 10
beta_one = 0.9
beta_two = 0.999
adam_eps = 1e-08

F32 = jnp.float32
BF16 = jnp.bfloat16

CHIP_GROUPS = [[2 * chip + core for chip in range(8)] for core in range(2)]
FF = 1792
VMEM = pltpu.VMEM


def fsdp_flip(value, flip):
    return lax.ppermute(value, "fsdp", [(i, i ^ flip) for i in range(16)])


def y_shift(value, dy):
    return lax.ppermute(value, "fsdp", [(i, (i + 4 * dy) % 16) for i in range(16)])


def tp_shift(value, dz, dh):
    pairs = [(i, ((i // 2 + dz) % 8) * 2 + ((i % 2) ^ dh)) for i in range(16)]
    return lax.ppermute(value, "tp", pairs)


SCALARS = pl.BlockSpec(memory_space=pltpu.SMEM)


def in_vmem(count):
    return [pl.BlockSpec(memory_space=VMEM)] * count


def local_call(kernel, name, out_shape, operands, flops, scratch=(), limit=24, aliases=None):
    size = sum(v.size * v.dtype.itemsize for v in operands)
    return pl.pallas_call(
        kernel,
        in_specs=[SCALARS] + in_vmem(len(operands) - 1),
        out_specs=in_vmem(len(out_shape)),
        out_shape=out_shape,
        scratch_shapes=scratch,
        input_output_aliases=aliases or {},
        cost_estimate=pl.CostEstimate(flops=flops, bytes_accessed=size, transcendentals=0),
        compiler_params=pltpu.CompilerParams(vmem_limit_bytes=limit << 20),
        name=name,
    )(*operands)


def front_kernel(where, a0, a1, a2, a3, p0, p1, p2, p3, o0, o1, o2, o3):
    low = where[0]
    total = None
    for r, p in enumerate((p0, p1, p2, p3)):
        columns = pl.ds(pl.multiple_of((low ^ r) * 512, 512), 512)
        rows = jnp.concatenate([a[:, columns] for a in (a0, a1, a2, a3)], axis=0)
        term = jnp.dot(rows, p[...], preferred_element_type=F32)
        total = term if total is None else total + term
    for i, o in enumerate((o0, o1, o2, o3)):
        o[...] = total[i * 64 : (i + 1) * 64]


def total_kernel(_, a, b, c, d, out):
    out[...] = (a[...] + b[...] + c[...] + d[...]).astype(BF16)


def join_kernel(where, mine, partner, out):
    first = where[20] == 0
    here, there = mine[...].astype(F32), partner[...].astype(F32)
    rows = jnp.concatenate(
        [jnp.where(first, here, there), jnp.where(first, there, here)], axis=0
    )
    out[...] = rows.T.astype(BF16)


def token_rows(where, grads, offset):
    row = lax.rem(where[1] + offset, 8) * 128
    return grads[pl.ds(pl.multiple_of(row, 128), 128), :]


def sum_kernel(offsets, where, *refs):
    count = len(offsets)
    blocks, grads, rest, out = refs[:count], refs[count], refs[count + 1 : -1], refs[-1]
    left = jnp.concatenate([b[...] for b in blocks], axis=1)
    right = jnp.concatenate([token_rows(where, grads, o) for o in offsets], axis=0)
    total = jnp.dot(left, right, preferred_element_type=F32)
    for before in rest:
        total = total + before[...]
    out[...] = total


def rows_from(table, start):
    low = lax.rem(start, 8)
    rows = table[pl.ds(pl.multiple_of(start - low, 8), 56), :]
    return pltpu.roll(rows, lax.rem(56 - low, 56), 0)[:48]


def last_kernel(offsets, where, *refs):
    give, keep, table = refs[-3:]
    table[512:560, :] = jnp.zeros((48, FF), F32)
    sum_kernel(offsets, where, *refs[:-3], table.at[0:512, :])
    core = where[2]
    for i in range(8):
        give[i] = rows_from(table, where[4 + 2 * i + 1 - core]).astype(give.dtype)
        keep[i] = rows_from(table, where[4 + 2 * i + core]).astype(keep.dtype)


def half_delta_kernel(_, chosen, updates, out):
    out[...] = jnp.dot(chosen[...], updates[...], preferred_element_type=F32)


def delta_kernel(_, chosen, updates, before, out):
    product = jnp.dot(chosen[...], updates[...], preferred_element_type=F32)
    out[...] = (before[...] + product).astype(BF16)


def moments_kernel(where, terms, first, second, new_first, new_second, spread):
    live = lax.broadcasted_iota(jnp.int32, (48, FF), 0) < where[3]
    gradient = terms[0].astype(F32)
    for i in range(1, 8):
        gradient = gradient + terms[i].astype(F32)
    one, two, update = adam_rows(gradient, live, first[...], second[...])
    new_first[...] = one
    new_second[...] = two
    for i in range(8):
        spread[i] = update


def adam_rows(gradient, live_mask, first_moment, second_moment):
    new_first = jnp.where(live_mask, beta_one * first_moment + (1.0 - beta_one) * gradient, 0.0)
    new_second = jnp.where(
        live_mask, beta_two * second_moment + (1.0 - beta_two) * gradient * gradient, 0.0
    )
    first_hat = new_first / (1.0 - beta_one**STEP)
    second_hat = new_second / (1.0 - beta_two**STEP)
    update = jnp.where(live_mask, first_hat / (jnp.sqrt(second_hat) + adam_eps), 0.0)
    return (new_first, new_second, update.astype(BF16))


def per_device(
    activations, grad_output, projection, piece_lengths, piece_owners, first_moment, second_moment
):
    tokens = activations[0]
    grads = grad_output[0]
    f = lax.axis_index("fsdp").astype(jnp.int32)
    c = lax.axis_index("tp").astype(jnp.int32)
    y, core = f // 4, f % 2
    z, h = c // 2, c % 2

    owner_order = jnp.arange(16, dtype=jnp.int32)
    starts = jnp.cumsum(piece_lengths) - piece_lengths
    matches = (piece_owners[None, :] == owner_order[:, None]).astype(jnp.int32)
    own_start = jnp.sum(matches * starts[None, :], axis=1)
    own_length = jnp.sum(matches * piece_lengths[None, :], axis=1)
    mine = jnp.sum(jnp.where(owner_order == f, own_length, 0))
    where = jnp.concatenate([jnp.stack([f % 4, z, core, mine]), own_start, h[None]]).astype(jnp.int32)
    offsets = jnp.arange(48, dtype=jnp.int32)
    rows = own_start[:, None] + offsets[None, :]
    live = offsets[None, :] < own_length[:, None]

    slices = [lax.dynamic_slice(tokens, (0, (y + s) % 4 * 2048), (64, 2048)) for s in range(4)]
    slices[1], slices[2], slices[3], block = lax.optimization_barrier(
        (slices[1], slices[2], slices[3], projection)
    )
    for s in (1, 3, 2):
        slices[s] = y_shift(slices[s], s)
    over_x = fsdp_flip(block, 2)
    over_core = fsdp_flip(block, 1)
    over_both = fsdp_flip(over_x, 1)

    over = (((1,), (1,)), ((), ()))

    def chosen_of(side):
        marks = jnp.where(live, rows, -1).reshape(8, 2, 48)
        marks = jnp.where(side == 0, marks[:, 0], marks[:, 1]).reshape(-1)
        hot = (marks[:, None] == jnp.arange(512, dtype=jnp.int32)[None, :]).astype(BF16)
        return lax.dot_general(projection, hot, over, preferred_element_type=F32).astype(BF16)

    same, cross = chosen_of(core), chosen_of(1 - core)
    same, cross, where, slices[2] = lax.optimization_barrier((same, cross, where, slices[2]))
    partial = local_call(
        front_kernel,
        "front",
        [jax.ShapeDtypeStruct((64, 512), F32)] * 4,
        (where, *slices, block, over_core, over_x, over_both),
        2 * 256 * 2048 * 512,
    )
    (projected,) = local_call(
        total_kernel,
        "total",
        [jax.ShapeDtypeStruct((64, 512), BF16)],
        (where, partial[0], *[y_shift(partial[s], -s) for s in (1, 3, 2)]),
        64 * 512 * 4,
        limit=4,
    )

    (own,) = local_call(
        join_kernel,
        "join",
        [jax.ShapeDtypeStruct((512, 128), BF16)],
        (where, projected, tp_shift(projected, 0, 1)),
        64 * 512 * 4,
        limit=4,
    )
    up1, down1 = tp_shift(own, 1, 0), tp_shift(own, -1, 0)
    up2, down2 = tp_shift(own, 2, 0), tp_shift(own, -2, 0)
    far = tp_shift(own, 4, 0)
    up3, down3 = tp_shift(up2, 1, 0), tp_shift(down2, -1, 0)
    table = [jax.ShapeDtypeStruct((512, FF), F32)]
    one = 2 * 512 * 128 * FF
    (gradient,) = local_call(
        functools.partial(sum_kernel, (0, 7, 1)),
        "near_terms",
        table,
        (where, own, up1, down1, grads),
        3 * one,
    )
    (gradient,) = local_call(
        functools.partial(sum_kernel, (6, 2, 4)),
        "far_terms",
        table,
        (where, up2, down2, far, grads, gradient),
        3 * one,
        aliases={5: 0},
    )
    give, keep = local_call(
        functools.partial(last_kernel, (5, 3)),
        "last_terms",
        [jax.ShapeDtypeStruct((8, 48, FF), BF16), jax.ShapeDtypeStruct((8, 48, FF), F32)],
        (where, up3, down3, grads, gradient),
        2 * one,
        scratch=[pltpu.VMEM((560, FF), F32)],
    )
    pair = (keep + fsdp_flip(give, 1).astype(F32)).astype(BF16)
    terms = lax.all_to_all(pair, "fsdp", 0, 0, axis_index_groups=CHIP_GROUPS)
    new_first, new_second, spread = local_call(
        moments_kernel,
        "moments",
        [
            jax.ShapeDtypeStruct((48, FF), F32),
            jax.ShapeDtypeStruct((48, FF), F32),
            jax.ShapeDtypeStruct((8, 48, FF), BF16),
        ],
        (where, terms, first_moment, second_moment),
        48 * FF * 30,
    )
    updates = lax.all_to_all(spread, "fsdp", 0, 0, axis_index_groups=CHIP_GROUPS)
    updates = updates.reshape(384, FF)
    crossed = fsdp_flip(updates, 1)
    (half,) = local_call(
        half_delta_kernel, "half_delta", table, (where, same, updates), 2 * 512 * 384 * FF
    )
    (weight_delta,) = local_call(
        delta_kernel,
        "delta",
        [jax.ShapeDtypeStruct((512, FF), BF16)],
        (where, cross, crossed, half),
        2 * 512 * 384 * FF,
    )
    return (weight_delta, new_first, new_second)


def solution(mesh):
    return jax.shard_map(
        per_device,
        mesh=mesh,
        in_specs=(
            P("fsdp", "tp", None),
            P("fsdp", None, "tp"),
            P("fsdp", None),
            P(),
            P(),
            P("fsdp", "tp"),
            P("fsdp", "tp"),
        ),
        out_specs=(P("fsdp", "tp"), P("fsdp", "tp"), P("fsdp", "tp")),
        check_vma=False,
    )
```

```python
import functools

import jax
import jax.numpy as jnp
from jax import lax
from jax.experimental import pallas as pl
from jax.experimental.pallas import tpu as pltpu
from jax.sharding import PartitionSpec as P

STEP = 10
beta_one = 0.9
beta_two = 0.999
adam_eps = 1e-08

F32 = jnp.float32
BF16 = jnp.bfloat16

LOW, Z, CORE, H, Y, X, F, START, LENGTH = 0, 1, 2, 3, 4, 5, 6, 16, 32
TO_CHIPS = [(1, 1), (3, 1), (2, 1), (1, 0), (3, 0), (0, 1), (2, 0), (0, 0)]
FROM_CHIPS = [(0, 0), (0, 1), (3, 0), (1, 0), (2, 0), (3, 1), (1, 1), (2, 1)]
FF = 1792
VMEM = pltpu.VMEM


def fsdp_flip(value, flip):
    return lax.ppermute(value, "fsdp", [(i, i ^ flip) for i in range(16)])


def y_shift(value, dy):
    return lax.ppermute(value, "fsdp", [(i, (i + 4 * dy) % 16) for i in range(16)])


def tp_shift(value, dz, dh):
    pairs = [(i, ((i // 2 + dz) % 8) * 2 + ((i % 2) ^ dh)) for i in range(16)]
    return lax.ppermute(value, "tp", pairs)


SCALARS = pl.BlockSpec(memory_space=pltpu.SMEM)
ANYWHERE = pl.BlockSpec(memory_space=pl.ANY)


def in_vmem(count):
    return [pl.BlockSpec(memory_space=VMEM)] * count


def local_call(
    kernel, name, out_shape, operands, flops, scratch=(), limit=24, aliases=None, anywhere=(0, 0)
):
    size = sum(v.size * v.dtype.itemsize for v in operands)
    return pl.pallas_call(
        kernel,
        in_specs=[SCALARS] + in_vmem(len(operands) - 1 - anywhere[0]) + [ANYWHERE] * anywhere[0],
        out_specs=in_vmem(len(out_shape) - anywhere[1]) + [ANYWHERE] * anywhere[1],
        out_shape=out_shape,
        scratch_shapes=scratch,
        input_output_aliases=aliases or {},
        cost_estimate=pl.CostEstimate(flops=flops, bytes_accessed=size, transcendentals=0),
        compiler_params=pltpu.CompilerParams(vmem_limit_bytes=limit << 20),
        name=name,
    )(*operands)


def table_kernel(lengths, owners, out):
    f = lax.axis_index("fsdp").astype(jnp.int32)
    c = lax.axis_index("tp").astype(jnp.int32)
    facts = {LOW: f % 4, Z: c // 2, CORE: f % 2, H: c % 2, Y: f // 4, X: f // 2 % 2, F: f}
    for place, value in facts.items():
        out[place] = value
    start = jnp.int32(0)
    for piece in range(16):
        owner = owners[piece]
        out[START + owner] = start
        out[LENGTH + owner] = lengths[piece]
        start = start + lengths[piece]


def scalar_table(lengths, owners):
    return pl.pallas_call(
        table_kernel,
        in_specs=[SCALARS] * 2,
        out_specs=SCALARS,
        out_shape=jax.ShapeDtypeStruct((48,), jnp.int32),
        cost_estimate=pl.CostEstimate(flops=0, bytes_accessed=512, transcendentals=0),
        compiler_params=pltpu.CompilerParams(vmem_limit_bytes=1 << 20),
        name="table",
    )(lengths, owners)


def owner_of(where, dy, dx, other):
    chip = lax.rem(where[Y] + dy, 4) * 2 + (where[X] ^ dx)
    return chip * 2 + (where[CORE] ^ other)


def choose_kernel(where, source, *refs):
    *outs, projection, semaphore = refs
    copy = pltpu.make_async_copy(source, projection, semaphore)
    copy.start()
    row = lax.broadcasted_iota(jnp.int32, (48, 512), 1)
    slot = lax.broadcasted_iota(jnp.int32, (48, 512), 0)
    for other, out in enumerate(outs):
        marks = []
        for dy, dx in FROM_CHIPS:
            owner = owner_of(where, dy, dx, other)
            live = (row == where[START + owner] + slot) & (slot < where[LENGTH + owner])
            marks.append(jnp.where(live, 1.0, 0.0))
        hot = jnp.concatenate(marks, axis=0).astype(BF16)
        if other == 0:
            copy.wait()
        out[...] = lax.dot_general(
            projection[...], hot, (((1,), (1,)), ((), ())), preferred_element_type=F32
        ).astype(BF16)


def token_product(where, r, tokens, block):
    columns = pl.ds(pl.multiple_of((where[LOW] ^ r) * 512, 512), 512)
    rows = jnp.concatenate([t[:, columns] for t in tokens], axis=0)
    return jnp.dot(rows, block[...], preferred_element_type=F32)


def front_kernel(where, a0, a1, a2, a3, p1, p2, p0, out, here, semaphore):
    copy = pltpu.make_async_copy(p0, here, semaphore)
    copy.start()
    tokens = (a0, a1, a2, a3)
    total = token_product(where, 1, tokens, p1) + token_product(where, 2, tokens, p2)
    copy.wait()
    out[...] = total + token_product(where, 0, tokens, here)


def front_rest_kernel(where, a0, a1, a2, a3, p3, before, o0, o1, o2, o3):
    total = before[...] + token_product(where, 3, (a0, a1, a2, a3), p3)
    for i, o in enumerate((o0, o1, o2, o3)):
        o[...] = total[i * 64 : (i + 1) * 64].astype(o.dtype)


def total_kernel(_, a, b, c, d, out):
    others = b[...].astype(F32) + c[...].astype(F32) + d[...].astype(F32)
    out[...] = (a[...] + others).astype(BF16)


def join_kernel(where, mine, partner, out):
    first = where[H] == 0
    here, there = mine[...].astype(F32), partner[...].astype(F32)
    rows = jnp.concatenate(
        [jnp.where(first, here, there), jnp.where(first, there, here)], axis=0
    )
    out[...] = rows.T.astype(BF16)


def token_rows(where, grads, offset):
    row = lax.rem(where[Z] + offset, 8) * 128
    return grads[pl.ds(pl.multiple_of(row, 128), 128), :]


def sum_kernel(offsets, where, *refs):
    count = len(offsets)
    blocks, grads, rest, out = refs[:count], refs[count], refs[count + 1 : -1], refs[-1]
    left = jnp.concatenate([b[...] for b in blocks], axis=1)
    right = jnp.concatenate([token_rows(where, grads, o) for o in offsets], axis=0)
    total = jnp.dot(left, right, preferred_element_type=F32)
    for before in rest:
        total = total + before[...]
    out[...] = total


def rows_from(table, start):
    low = lax.rem(start, 8)
    rows = table[pl.ds(pl.multiple_of(start - low, 8), 56), :]
    return pltpu.roll(rows, lax.rem(56 - low, 56), 0)[:48]


def last_kernel(offsets, where, *refs):
    give, keep, table = refs[-3:]
    table[512:560, :] = jnp.zeros((48, FF), F32)
    sum_kernel(offsets, where, *refs[:-3], table.at[0:512, :])
    for i, (dy, dx) in enumerate(TO_CHIPS):
        give[i] = rows_from(table, where[START + owner_of(where, dy, dx, 1)]).astype(BF16)
        keep[i] = rows_from(table, where[START + owner_of(where, dy, dx, 0)])


def pair_kernel(_, keep, given, *outs):
    for i, out in enumerate(outs):
        out[...] = (keep[i] + given[i].astype(F32)).astype(out.dtype)


def add_kernel(_, *refs):
    total = refs[0][...]
    for r in refs[1:-1]:
        total = total + r[...].astype(F32)
    refs[-1][...] = total.astype(BF16)


def moments_kernel(where, own, t1, t2, t3, t4, first, second, new_first, new_second, update):
    live = lax.broadcasted_iota(jnp.int32, (48, FF), 0) < where[LENGTH + where[F]]
    gradient = own[...]
    for t in (t1, t2, t3, t4):
        gradient = gradient + t[...].astype(F32)
    one, two, three = adam_rows(gradient, live, first[...], second[...])
    new_first[...] = one
    new_second[...] = two
    update[...] = three


def half_delta_kernel(_, chosen, updates, out):
    out[...] = jnp.dot(chosen[...], updates[...], preferred_element_type=F32)


def delta_kernel(_, chosen, updates, before, out, whole, semaphores):
    copies = []
    for i in range(7):
        columns = slice(256 * i, 256 * i + 256)
        product = jnp.dot(chosen[...], updates[:, columns], preferred_element_type=F32)
        whole[:, columns] = (before[:, columns] + product).astype(BF16)
        copy = pltpu.make_async_copy(
            whole.at[:, pl.ds(256 * i, 256)], out.at[:, pl.ds(256 * i, 256)], semaphores.at[i]
        )
        copy.start()
        copies.append(copy)
    for copy in copies:
        copy.wait()


def adam_rows(gradient, live_mask, first_moment, second_moment):
    new_first = jnp.where(live_mask, beta_one * first_moment + (1.0 - beta_one) * gradient, 0.0)
    new_second = jnp.where(
        live_mask, beta_two * second_moment + (1.0 - beta_two) * gradient * gradient, 0.0
    )
    first_hat = new_first / (1.0 - beta_one**STEP)
    second_hat = new_second / (1.0 - beta_two**STEP)
    update = jnp.where(live_mask, first_hat / (jnp.sqrt(second_hat) + adam_eps), 0.0)
    return (new_first, new_second, update.astype(BF16))


def per_device(
    activations, grad_output, projection, piece_lengths, piece_owners, first_moment, second_moment
):
    tokens = activations[0]
    grads = grad_output[0]
    y = lax.axis_index("fsdp").astype(jnp.int32) // 4
    slices = [lax.dynamic_slice(tokens, (0, (y + s) % 4 * 2048), (64, 2048)) for s in range(4)]
    *slices[1:], block, lengths = lax.optimization_barrier(
        (*slices[1:], projection, piece_lengths)
    )
    where = scalar_table(lengths, piece_owners)
    for s in (1, 3, 2):
        slices[s] = y_shift(slices[s], s)
    over_x = fsdp_flip(block, 2)
    over_core = fsdp_flip(block, 1)

    chosen = local_call(
        choose_kernel,
        "choose",
        [jax.ShapeDtypeStruct((512, 384), BF16)] * 2,
        (where, projection),
        2 * 512 * 512 * 768,
        scratch=[pltpu.VMEM((512, 512), BF16), pltpu.SemaphoreType.DMA],
        limit=8,
        anywhere=(1, 0),
    )
    over_x, where, *slices[1:] = lax.optimization_barrier((over_x, where, *slices[1:]))
    over_both = fsdp_flip(over_x, 1)
    (partial,) = local_call(
        front_kernel,
        "front",
        [jax.ShapeDtypeStruct((256, 512), F32)],
        (where, *slices, over_core, over_x, block),
        2 * 256 * 1536 * 512,
        scratch=[pltpu.VMEM((512, 512), BF16), pltpu.SemaphoreType.DMA],
        limit=8,
        anywhere=(1, 0),
    )
    mine, *partial = local_call(
        front_rest_kernel,
        "front_rest",
        [jax.ShapeDtypeStruct((64, 512), F32)] + [jax.ShapeDtypeStruct((64, 512), BF16)] * 3,
        (where, *slices, over_both, partial),
        2 * 256 * 512 * 512,
        limit=8,
    )
    same, cross, mine = lax.optimization_barrier((*chosen, mine))
    (projected,) = local_call(
        total_kernel,
        "total",
        [jax.ShapeDtypeStruct((64, 512), BF16)],
        (where, mine, *[y_shift(partial[s - 1], -s) for s in (1, 3, 2)]),
        64 * 512 * 4,
        limit=4,
    )

    (own,) = local_call(
        join_kernel,
        "join",
        [jax.ShapeDtypeStruct((512, 128), BF16)],
        (where, projected, tp_shift(projected, 0, 1)),
        64 * 512 * 4,
        limit=4,
    )
    up1, down1 = tp_shift(own, 1, 0), tp_shift(own, -1, 0)
    far = tp_shift(own, 4, 0)
    up2, down2 = tp_shift(up1, 1, 0), tp_shift(down1, -1, 0)
    table = [jax.ShapeDtypeStruct((512, FF), F32)]
    one = 2 * 512 * 128 * FF
    (gradient,) = local_call(
        functools.partial(sum_kernel, (0, 7, 1)),
        "near_terms",
        table,
        (where, own, up1, down1, grads),
        3 * one,
    )
    up2, down2, gradient = lax.optimization_barrier((up2, down2, gradient))
    up3, down3 = tp_shift(up2, 1, 0), tp_shift(down2, -1, 0)
    (gradient,) = local_call(
        functools.partial(sum_kernel, (6, 2)),
        "middle_terms",
        table,
        (where, up2, down2, grads, gradient),
        2 * one,
        aliases={4: 0},
    )
    give, keep = local_call(
        functools.partial(last_kernel, (5, 3, 4)),
        "last_terms",
        [
            jax.ShapeDtypeStruct((8, 48, FF), BF16),
            jax.ShapeDtypeStruct((8, 48, FF), F32),
        ],
        (where, up3, down3, far, grads, gradient),
        3 * one,
        scratch=[pltpu.VMEM((560, FF), F32)],
    )

    narrow, wide = jax.ShapeDtypeStruct((48, FF), BF16), jax.ShapeDtypeStruct((48, FF), F32)
    size = 48 * FF
    up_x, down_x, far_x, up, down, beside, far, mine = local_call(
        pair_kernel,
        "pair",
        [narrow] * 5 + [wide] * 3,
        (where, keep, fsdp_flip(give, 1)),
        8 * size,
        limit=8,
    )
    up_x, down_x, far_x = y_shift(up_x, 1), y_shift(down_x, -1), fsdp_flip(far_x, 2)
    up, down = y_shift(up, 1), y_shift(down, -1)
    (far,) = local_call(add_kernel, "add_far", [narrow], (where, far, far_x), size, limit=8)
    far, up, down = lax.optimization_barrier((far, up, down))
    far = y_shift(far, 2)
    (beside,) = local_call(
        add_kernel, "add_beside", [narrow], (where, beside, up_x, down_x), 2 * size, limit=8
    )
    beside = fsdp_flip(beside, 2)
    new_first, new_second, update = local_call(
        moments_kernel,
        "moments",
        [wide, wide, narrow],
        (where, mine, up, down, far, beside, first_moment, second_moment),
        30 * size,
        limit=8,
    )

    beside = fsdp_flip(update, 2)
    up, down, far = y_shift(update, 1), y_shift(update, -1), y_shift(update, 2)
    up_x, down_x, far_x = y_shift(beside, 1), y_shift(beside, -1), fsdp_flip(far, 2)
    updates = jnp.concatenate([update, beside, up, down, far, up_x, down_x, far_x], axis=0)
    crossed = fsdp_flip(updates, 1)
    (delta,) = local_call(
        half_delta_kernel, "half_delta", table, (where, same, updates), 2 * 512 * 384 * FF
    )
    (weight_delta,) = local_call(
        delta_kernel,
        "delta",
        [jax.ShapeDtypeStruct((512, FF), BF16)],
        (where, cross, crossed, delta),
        2 * 512 * 384 * FF,
        scratch=[pltpu.VMEM((512, FF), BF16), pltpu.SemaphoreType.DMA((7,))],
        anywhere=(0, 1),
    )
    return (weight_delta, new_first, new_second)


def solution(mesh):
    return jax.shard_map(
        per_device,
        mesh=mesh,
        in_specs=(
            P("fsdp", "tp", None),
            P("fsdp", None, "tp"),
            P("fsdp", None),
            P(),
            P(),
            P("fsdp", "tp"),
            P("fsdp", "tp"),
        ),
        out_specs=(P("fsdp", "tp"), P("fsdp", "tp"), P("fsdp", "tp")),
        check_vma=False,
    )
```

```python
import functools

import jax
import jax.numpy as jnp
from jax import lax
from jax.experimental import pallas as pl
from jax.experimental.pallas import tpu as pltpu
from jax.sharding import PartitionSpec as P

STEP = 10
beta_one = 0.9
beta_two = 0.999
adam_eps = 1e-08

F32 = jnp.float32
BF16 = jnp.bfloat16

LOW, Z, CORE, H, Y, X, F, START, LENGTH = 0, 1, 2, 3, 4, 5, 6, 16, 32
TO_CHIPS = [(1, 1), (3, 1), (2, 1), (1, 0), (3, 0), (0, 1), (2, 0), (0, 0)]
FROM_CHIPS = [(0, 0), (0, 1), (3, 0), (1, 0), (2, 0), (3, 1), (1, 1), (2, 1)]
FF = 1792
VMEM = pltpu.VMEM


def fsdp_flip(value, flip):
    return lax.ppermute(value, "fsdp", [(i, i ^ flip) for i in range(16)])


def y_shift(value, dy):
    return lax.ppermute(value, "fsdp", [(i, (i + 4 * dy) % 16) for i in range(16)])


def tp_shift(value, dz, dh):
    pairs = [(i, ((i // 2 + dz) % 8) * 2 + ((i % 2) ^ dh)) for i in range(16)]
    return lax.ppermute(value, "tp", pairs)


SCALARS = pl.BlockSpec(memory_space=pltpu.SMEM)
ANYWHERE = pl.BlockSpec(memory_space=pl.ANY)


def in_vmem(count):
    return [pl.BlockSpec(memory_space=VMEM)] * count


def local_call(
    kernel, name, out_shape, operands, flops, scratch=(), limit=24, aliases=None, anywhere=(0, 0), cheap=False
):
    size = sum(v.size * v.dtype.itemsize for v in operands)
    if cheap:
        flops, size = 1 << 10, 1 << 10
    return pl.pallas_call(
        kernel,
        in_specs=[SCALARS] + in_vmem(len(operands) - 1 - anywhere[0]) + [ANYWHERE] * anywhere[0],
        out_specs=in_vmem(len(out_shape) - anywhere[1]) + [ANYWHERE] * anywhere[1],
        out_shape=out_shape,
        scratch_shapes=scratch,
        input_output_aliases=aliases or {},
        cost_estimate=pl.CostEstimate(flops=flops, bytes_accessed=size, transcendentals=0),
        compiler_params=pltpu.CompilerParams(vmem_limit_bytes=limit << 20),
        name=name,
    )(*operands)


def table_kernel(lengths, owners, out):
    f = lax.axis_index("fsdp").astype(jnp.int32)
    c = lax.axis_index("tp").astype(jnp.int32)
    facts = {LOW: f % 4, Z: c // 2, CORE: f % 2, H: c % 2, Y: f // 4, X: f // 2 % 2, F: f}
    for place, value in facts.items():
        out[place] = value
    start = jnp.int32(0)
    for piece in range(16):
        owner = owners[piece]
        out[START + owner] = start
        out[LENGTH + owner] = lengths[piece]
        start = start + lengths[piece]


def scalar_table(lengths, owners):
    return pl.pallas_call(
        table_kernel,
        in_specs=[SCALARS] * 2,
        out_specs=SCALARS,
        out_shape=jax.ShapeDtypeStruct((48,), jnp.int32),
        cost_estimate=pl.CostEstimate(flops=0, bytes_accessed=512, transcendentals=0),
        compiler_params=pltpu.CompilerParams(vmem_limit_bytes=1 << 20),
        name="table",
    )(lengths, owners)


def owner_of(where, dy, dx, other):
    chip = lax.rem(where[Y] + dy, 4) * 2 + (where[X] ^ dx)
    return chip * 2 + (where[CORE] ^ other)


def choose_kernel(where, source, *refs):
    *outs, projection, semaphore = refs
    copy = pltpu.make_async_copy(source, projection, semaphore)
    copy.start()
    row = lax.broadcasted_iota(jnp.int32, (48, 512), 1)
    slot = lax.broadcasted_iota(jnp.int32, (48, 512), 0)
    for other, out in enumerate(outs):
        marks = []
        for dy, dx in FROM_CHIPS:
            owner = owner_of(where, dy, dx, other)
            live = (row == where[START + owner] + slot) & (slot < where[LENGTH + owner])
            marks.append(jnp.where(live, 1.0, 0.0))
        hot = jnp.concatenate(marks, axis=0).astype(BF16)
        if other == 0:
            copy.wait()
        out[...] = lax.dot_general(
            projection[...], hot, (((1,), (1,)), ((), ())), preferred_element_type=F32
        ).astype(BF16)


def token_product(where, r, tokens, block):
    columns = pl.ds(pl.multiple_of((where[LOW] ^ r) * 512, 512), 512)
    rows = jnp.concatenate([t[:, columns] for t in tokens], axis=0)
    return jnp.dot(rows, block[...], preferred_element_type=F32)


def front_kernel(where, a0, a1, a2, a3, p1, p2, p0, out, here, semaphore):
    copy = pltpu.make_async_copy(p0, here, semaphore)
    copy.start()
    tokens = (a0, a1, a2, a3)
    total = token_product(where, 1, tokens, p1) + token_product(where, 2, tokens, p2)
    copy.wait()
    out[...] = total + token_product(where, 0, tokens, here)


def front_rest_kernel(where, a0, a1, a2, a3, p3, before, o0, o1, o2, o3):
    total = before[...] + token_product(where, 3, (a0, a1, a2, a3), p3)
    for i, o in enumerate((o0, o1, o2, o3)):
        o[...] = total[i * 64 : (i + 1) * 64].astype(o.dtype)


def total_kernel(_, a, b, c, d, out):
    others = b[...].astype(F32) + c[...].astype(F32) + d[...].astype(F32)
    out[...] = (a[...] + others).astype(BF16)


def join_kernel(where, mine, partner, out):
    first = where[H] == 0
    here, there = mine[...].astype(F32), partner[...].astype(F32)
    rows = jnp.concatenate(
        [jnp.where(first, here, there), jnp.where(first, there, here)], axis=0
    )
    out[...] = rows.T.astype(BF16)


def token_rows(where, grads, offset):
    row = lax.rem(where[Z] + offset, 8) * 128
    return grads[pl.ds(pl.multiple_of(row, 128), 128), :]


def sum_kernel(offsets, where, *refs):
    count = len(offsets)
    blocks, grads, rest, out = refs[:count], refs[count], refs[count + 1 : -1], refs[-1]
    left = jnp.concatenate([b[...] for b in blocks], axis=1)
    right = jnp.concatenate([token_rows(where, grads, o) for o in offsets], axis=0)
    total = jnp.dot(left, right, preferred_element_type=F32)
    for before in rest:
        total = total + before[...]
    out[...] = total


def rows_from(table, start):
    low = lax.rem(start, 8)
    rows = table[pl.ds(pl.multiple_of(start - low, 8), 56), :]
    return pltpu.roll(rows, lax.rem(56 - low, 56), 0)[:48]


def last_kernel(offsets, where, *refs):
    give, keep, table = refs[-3:]
    table[512:560, :] = jnp.zeros((48, FF), F32)
    sum_kernel(offsets, where, *refs[:-3], table.at[0:512, :])
    for i, (dy, dx) in enumerate(TO_CHIPS):
        give[i] = rows_from(table, where[START + owner_of(where, dy, dx, 1)]).astype(BF16)
        keep[i] = rows_from(table, where[START + owner_of(where, dy, dx, 0)])


def pair_kernel(first, _, keep, given, *outs):
    for i, out in enumerate(outs, first):
        out[...] = (keep[i] + given[i].astype(F32)).astype(out.dtype)


def add_kernel(_, *refs):
    total = refs[0][...]
    for r in refs[1:-1]:
        total = total + r[...].astype(F32)
    refs[-1][...] = total.astype(refs[-1].dtype)


def update_kernel(where, own, t1, t2, first, second, update, gradient):
    live = lax.broadcasted_iota(jnp.int32, (48, FF), 0) < where[LENGTH + where[F]]
    total = own[...]
    for t in (t1, t2):
        total = total + t[...].astype(F32)
    gradient[...] = total
    update[...] = adam_rows(total, live, first[...], second[...])[2]


def moments_kernel(where, update, gradient, first, second, again, new_first, new_second):
    live = lax.broadcasted_iota(jnp.int32, (48, FF), 0) < where[LENGTH + where[F]]
    again[...] = update[...]
    one, two, _ = adam_rows(gradient[...], live, first[...], second[...])
    new_first[...] = one
    new_second[...] = two


def half_delta_kernel(_, chosen, updates, out):
    out[...] = jnp.dot(chosen[...], updates[...], preferred_element_type=F32)


def delta_kernel(_, chosen, updates, before, out, whole, semaphores):
    copies = []
    for i in range(7):
        columns = slice(256 * i, 256 * i + 256)
        product = jnp.dot(chosen[...], updates[:, columns], preferred_element_type=F32)
        whole[:, columns] = (before[:, columns] + product).astype(BF16)
        copy = pltpu.make_async_copy(
            whole.at[:, pl.ds(256 * i, 256)], out.at[:, pl.ds(256 * i, 256)], semaphores.at[i]
        )
        copy.start()
        copies.append(copy)
    for copy in copies:
        copy.wait()


def adam_rows(gradient, live_mask, first_moment, second_moment):
    new_first = jnp.where(live_mask, beta_one * first_moment + (1.0 - beta_one) * gradient, 0.0)
    new_second = jnp.where(
        live_mask, beta_two * second_moment + (1.0 - beta_two) * gradient * gradient, 0.0
    )
    first_hat = new_first / (1.0 - beta_one**STEP)
    second_hat = new_second / (1.0 - beta_two**STEP)
    update = jnp.where(live_mask, first_hat / (jnp.sqrt(second_hat) + adam_eps), 0.0)
    return (new_first, new_second, update.astype(BF16))


def per_device(
    activations, grad_output, projection, piece_lengths, piece_owners, first_moment, second_moment
):
    tokens = activations[0]
    grads = grad_output[0]
    y = lax.axis_index("fsdp").astype(jnp.int32) // 4
    slices = [lax.dynamic_slice(tokens, (0, (y + s) % 4 * 2048), (64, 2048)) for s in range(4)]
    *slices[1:], block, lengths = lax.optimization_barrier(
        (*slices[1:], projection, piece_lengths)
    )
    where = scalar_table(lengths, piece_owners)
    for s in (1, 3, 2):
        slices[s] = y_shift(slices[s], s)
    over_x = fsdp_flip(block, 2)
    over_core = fsdp_flip(block, 1)

    chosen = local_call(
        choose_kernel,
        "choose",
        [jax.ShapeDtypeStruct((512, 384), BF16)] * 2,
        (where, projection),
        2 * 512 * 512 * 768,
        scratch=[pltpu.VMEM((512, 512), BF16), pltpu.SemaphoreType.DMA],
        limit=8,
        anywhere=(1, 0),
    )
    over_x, where, *slices[1:] = lax.optimization_barrier((over_x, where, *slices[1:]))
    over_both = fsdp_flip(over_x, 1)
    (partial,) = local_call(
        front_kernel,
        "front",
        [jax.ShapeDtypeStruct((256, 512), F32)],
        (where, *slices, over_core, over_x, block),
        2 * 256 * 1536 * 512,
        scratch=[pltpu.VMEM((512, 512), BF16), pltpu.SemaphoreType.DMA],
        limit=8,
        anywhere=(1, 0),
    )
    mine, *partial = local_call(
        front_rest_kernel,
        "front_rest",
        [jax.ShapeDtypeStruct((64, 512), F32)] + [jax.ShapeDtypeStruct((64, 512), BF16)] * 3,
        (where, *slices, over_both, partial),
        2 * 256 * 512 * 512,
        limit=8,
    )
    same, cross, mine = lax.optimization_barrier((*chosen, mine))
    (projected,) = local_call(
        total_kernel,
        "total",
        [jax.ShapeDtypeStruct((64, 512), BF16)],
        (where, mine, *[y_shift(partial[s - 1], -s) for s in (1, 3, 2)]),
        64 * 512 * 4,
        limit=4,
    )

    (own,) = local_call(
        join_kernel,
        "join",
        [jax.ShapeDtypeStruct((512, 128), BF16)],
        (where, projected, tp_shift(projected, 0, 1)),
        64 * 512 * 4,
        limit=4,
    )
    up1, down1 = tp_shift(own, 1, 0), tp_shift(own, -1, 0)
    far = tp_shift(own, 4, 0)
    up2, down2 = tp_shift(up1, 1, 0), tp_shift(down1, -1, 0)
    table = [jax.ShapeDtypeStruct((512, FF), F32)]
    one = 2 * 512 * 128 * FF
    (gradient,) = local_call(
        functools.partial(sum_kernel, (0, 7, 1)),
        "near_terms",
        table,
        (where, own, up1, down1, grads),
        3 * one,
        cheap=True,
    )
    up2, down2, gradient = lax.optimization_barrier((up2, down2, gradient))
    up3, down3 = tp_shift(up2, 1, 0), tp_shift(down2, -1, 0)
    (gradient,) = local_call(
        functools.partial(sum_kernel, (6, 2)),
        "middle_terms",
        table,
        (where, up2, down2, grads, gradient),
        2 * one,
        aliases={4: 0},
        cheap=True,
    )
    give, keep = local_call(
        functools.partial(last_kernel, (5, 3, 4)),
        "last_terms",
        [
            jax.ShapeDtypeStruct((8, 48, FF), BF16),
            jax.ShapeDtypeStruct((8, 48, FF), F32),
        ],
        (where, up3, down3, far, grads, gradient),
        3 * one,
        scratch=[pltpu.VMEM((560, FF), F32)],
    )

    narrow, wide = jax.ShapeDtypeStruct((48, FF), BF16), jax.ShapeDtypeStruct((48, FF), F32)
    size = 48 * FF
    given = fsdp_flip(give, 1)
    up_x, down_x, far_x = local_call(
        functools.partial(pair_kernel, 0),
        "pair_first",
        [narrow] * 3,
        (where, keep, given),
        3 * size,
        limit=8,
    )
    up_x, down_x, far_x = y_shift(up_x, 1), y_shift(down_x, -1), fsdp_flip(far_x, 2)
    up, down, beside, far, mine = local_call(
        functools.partial(pair_kernel, 3),
        "pair_rest",
        [narrow] * 2 + [wide] * 3,
        (where, keep, given),
        5 * size,
        limit=8,
    )
    up, down = y_shift(up, 1), y_shift(down, -1)
    (far,) = local_call(add_kernel, "add_far", [narrow], (where, far, far_x), size, limit=8)
    far = y_shift(far, 2)
    (mine,) = local_call(
        add_kernel, "add_direct", [wide], (where, mine, up, down), 2 * size, limit=8
    )
    (beside,) = local_call(
        add_kernel, "add_beside", [narrow], (where, beside, up_x, down_x), 2 * size, limit=8
    )
    beside = fsdp_flip(beside, 2)
    update, gradient = local_call(
        update_kernel,
        "update",
        [narrow, wide],
        (where, mine, far, beside, first_moment, second_moment),
        30 * size,
        limit=8,
    )

    beside = fsdp_flip(update, 2)
    update, new_first, new_second = local_call(
        moments_kernel,
        "moments",
        [narrow, wide, wide],
        (where, update, gradient, first_moment, second_moment),
        30 * size,
        limit=8,
    )
    up, down, far = y_shift(update, 1), y_shift(update, -1), y_shift(update, 2)
    up_x, down_x, far_x = y_shift(beside, 1), y_shift(beside, -1), fsdp_flip(far, 2)
    updates = jnp.concatenate([update, beside, up, down, far, up_x, down_x, far_x], axis=0)
    crossed = fsdp_flip(updates, 1)
    (delta,) = local_call(
        half_delta_kernel, "half_delta", table, (where, same, updates), 2 * 512 * 384 * FF
    )
    (weight_delta,) = local_call(
        delta_kernel,
        "delta",
        [jax.ShapeDtypeStruct((512, FF), BF16)],
        (where, cross, crossed, delta),
        2 * 512 * 384 * FF,
        scratch=[pltpu.VMEM((512, FF), BF16), pltpu.SemaphoreType.DMA((7,))],
        anywhere=(0, 1),
    )
    return (weight_delta, new_first, new_second)


def solution(mesh):
    return jax.shard_map(
        per_device,
        mesh=mesh,
        in_specs=(
            P("fsdp", "tp", None),
            P("fsdp", None, "tp"),
            P("fsdp", None),
            P(),
            P(),
            P("fsdp", "tp"),
            P("fsdp", "tp"),
        ),
        out_specs=(P("fsdp", "tp"), P("fsdp", "tp"), P("fsdp", "tp")),
        check_vma=False,
    )
```

```python
import functools

import jax
import jax.numpy as jnp
from jax import lax
from jax.experimental import pallas as pl
from jax.experimental.pallas import tpu as pltpu
from jax.sharding import PartitionSpec as P

STEP = 10
beta_one = 0.9
beta_two = 0.999
adam_eps = 1e-08

F32 = jnp.float32
BF16 = jnp.bfloat16

LOW, Z, CORE, H, Y, X, F, START, LENGTH = 0, 1, 2, 3, 4, 5, 6, 16, 32
TO_CHIPS = [(1, 1), (3, 1), (2, 1), (1, 0), (3, 0), (0, 1), (2, 0), (0, 0)]
FROM_CHIPS = [(0, 0), (0, 1), (3, 0), (1, 0), (2, 0), (3, 1), (1, 1), (2, 1)]
FF = 1792
VMEM = pltpu.VMEM


def fsdp_flip(value, flip):
    return lax.ppermute(value, "fsdp", [(i, i ^ flip) for i in range(16)])


def y_shift(value, dy):
    return lax.ppermute(value, "fsdp", [(i, (i + 4 * dy) % 16) for i in range(16)])


def tp_shift(value, dz, dh):
    pairs = [(i, ((i // 2 + dz) % 8) * 2 + ((i % 2) ^ dh)) for i in range(16)]
    return lax.ppermute(value, "tp", pairs)


SCALARS = pl.BlockSpec(memory_space=pltpu.SMEM)
ANYWHERE = pl.BlockSpec(memory_space=pl.ANY)


def in_vmem(count):
    return [pl.BlockSpec(memory_space=VMEM)] * count


def local_call(
    kernel, name, out_shape, operands, flops, scratch=(), limit=24, aliases=None, anywhere=(0, 0), cheap=False
):
    size = sum(v.size * v.dtype.itemsize for v in operands)
    if cheap:
        flops, size = 1 << 10, 1 << 10
    return pl.pallas_call(
        kernel,
        in_specs=[SCALARS] + in_vmem(len(operands) - 1 - anywhere[0]) + [ANYWHERE] * anywhere[0],
        out_specs=in_vmem(len(out_shape) - anywhere[1]) + [ANYWHERE] * anywhere[1],
        out_shape=out_shape,
        scratch_shapes=scratch,
        input_output_aliases=aliases or {},
        cost_estimate=pl.CostEstimate(flops=flops, bytes_accessed=size, transcendentals=0),
        compiler_params=pltpu.CompilerParams(vmem_limit_bytes=limit << 20),
        name=name,
    )(*operands)


def table_kernel(lengths, owners, out):
    f = lax.axis_index("fsdp").astype(jnp.int32)
    c = lax.axis_index("tp").astype(jnp.int32)
    facts = {LOW: f % 4, Z: c // 2, CORE: f % 2, H: c % 2, Y: f // 4, X: f // 2 % 2, F: f}
    for place, value in facts.items():
        out[place] = value
    start = jnp.int32(0)
    for piece in range(16):
        owner = owners[piece]
        out[START + owner] = start
        out[LENGTH + owner] = lengths[piece]
        start = start + lengths[piece]


def scalar_table(lengths, owners):
    return pl.pallas_call(
        table_kernel,
        in_specs=[SCALARS] * 2,
        out_specs=SCALARS,
        out_shape=jax.ShapeDtypeStruct((48,), jnp.int32),
        cost_estimate=pl.CostEstimate(flops=0, bytes_accessed=512, transcendentals=0),
        compiler_params=pltpu.CompilerParams(vmem_limit_bytes=1 << 20),
        name="table",
    )(lengths, owners)


def owner_of(where, dy, dx, other):
    chip = lax.rem(where[Y] + dy, 4) * 2 + (where[X] ^ dx)
    return chip * 2 + (where[CORE] ^ other)


def choose_kernel(where, source, *refs):
    *outs, projection, semaphore = refs
    copy = pltpu.make_async_copy(source, projection, semaphore)
    copy.start()
    row = lax.broadcasted_iota(jnp.int32, (48, 512), 1)
    slot = lax.broadcasted_iota(jnp.int32, (48, 512), 0)
    for other, out in enumerate(outs):
        marks = []
        for dy, dx in FROM_CHIPS:
            owner = owner_of(where, dy, dx, other)
            live = (row == where[START + owner] + slot) & (slot < where[LENGTH + owner])
            marks.append(jnp.where(live, 1.0, 0.0))
        hot = jnp.concatenate(marks, axis=0).astype(BF16)
        if other == 0:
            copy.wait()
        out[...] = lax.dot_general(
            projection[...], hot, (((1,), (1,)), ((), ())), preferred_element_type=F32
        ).astype(BF16)


def token_product(where, r, tokens, block):
    columns = pl.ds(pl.multiple_of((where[LOW] ^ r) * 512, 512), 512)
    rows = jnp.concatenate([t[:, columns] for t in tokens], axis=0)
    return jnp.dot(rows, block[...], preferred_element_type=F32)


def front_kernel(where, a0, a1, a2, a3, p1, p2, p0, out, here, semaphore):
    copy = pltpu.make_async_copy(p0, here, semaphore)
    copy.start()
    tokens = (a0, a1, a2, a3)
    total = token_product(where, 1, tokens, p1) + token_product(where, 2, tokens, p2)
    copy.wait()
    out[...] = total + token_product(where, 0, tokens, here)


def front_rest_kernel(where, a0, a1, a2, a3, p3, before, o0, o1, o2, o3):
    total = before[...] + token_product(where, 3, (a0, a1, a2, a3), p3)
    for i, o in enumerate((o0, o1, o2, o3)):
        o[...] = total[i * 64 : (i + 1) * 64].astype(o.dtype)


def total_kernel(_, a, b, c, d, out):
    others = b[...].astype(F32) + c[...].astype(F32) + d[...].astype(F32)
    out[...] = (a[...] + others).astype(BF16)


def join_kernel(where, mine, partner, out):
    first = where[H] == 0
    here, there = mine[...].astype(F32), partner[...].astype(F32)
    rows = jnp.concatenate(
        [jnp.where(first, here, there), jnp.where(first, there, here)], axis=0
    )
    out[...] = rows.T.astype(BF16)


def token_rows(where, grads, offset):
    row = lax.rem(where[Z] + offset, 8) * 128
    return grads[pl.ds(pl.multiple_of(row, 128), 128), :]


def sum_kernel(offsets, where, *refs):
    count = len(offsets)
    blocks, grads, rest, out = refs[:count], refs[count], refs[count + 1 : -1], refs[-1]
    left = jnp.concatenate([b[...] for b in blocks], axis=1)
    right = jnp.concatenate([token_rows(where, grads, o) for o in offsets], axis=0)
    total = jnp.dot(left, right, preferred_element_type=F32)
    for before in rest:
        total = total + before[...]
    out[...] = total


def rows_from(table, start):
    low = lax.rem(start, 8)
    rows = table[pl.ds(pl.multiple_of(start - low, 8), 56), :]
    return pltpu.roll(rows, lax.rem(56 - low, 56), 0)[:48]


def last_kernel(offsets, where, *refs):
    give, table = refs[-2:]
    table[512:560, :] = jnp.zeros((48, FF), F32)
    sum_kernel(offsets, where, *refs[:-2], table.at[0:512, :])
    for i, (dy, dx) in enumerate(TO_CHIPS):
        give[i] = rows_from(table, where[START + owner_of(where, dy, dx, 1)]).astype(BF16)


def keep_kernel(where, table, keep):
    for i, (dy, dx) in enumerate(TO_CHIPS):
        keep[i] = rows_from(table, where[START + owner_of(where, dy, dx, 0)])


def pair_kernel(first, _, keep, given, *outs):
    for i, out in enumerate(outs, first):
        out[...] = (keep[i] + given[i].astype(F32)).astype(out.dtype)


def add_kernel(_, *refs):
    total = refs[0][...]
    for r in refs[1:-1]:
        total = total + r[...].astype(F32)
    refs[-1][...] = total.astype(refs[-1].dtype)


def update_kernel(where, own, t1, t2, first, second, update, gradient):
    live = lax.broadcasted_iota(jnp.int32, (48, FF), 0) < where[LENGTH + where[F]]
    total = own[...]
    for t in (t1, t2):
        total = total + t[...].astype(F32)
    gradient[...] = total
    update[...] = adam_rows(total, live, first[...], second[...])[2]


def first_kernel(where, update, gradient, first, again, new_first):
    live = lax.broadcasted_iota(jnp.int32, (48, FF), 0) < where[LENGTH + where[F]]
    again[...] = update[...]
    new_first[...] = adam_rows(gradient[...], live, first[...], jnp.zeros((48, FF), F32))[0]


def second_kernel(where, gradient, second, new_second):
    live = lax.broadcasted_iota(jnp.int32, (48, FF), 0) < where[LENGTH + where[F]]
    new_second[...] = adam_rows(gradient[...], live, jnp.zeros((48, FF), F32), second[...])[1]


def half_delta_kernel(_, chosen, updates, out):
    out[...] = jnp.dot(chosen[...], updates[...], preferred_element_type=F32)


def delta_kernel(_, chosen, updates, before, out, whole, semaphores):
    copies = []
    for i in range(7):
        columns = slice(256 * i, 256 * i + 256)
        product = jnp.dot(chosen[...], updates[:, columns], preferred_element_type=F32)
        whole[:, columns] = (before[:, columns] + product).astype(BF16)
        copy = pltpu.make_async_copy(
            whole.at[:, pl.ds(256 * i, 256)], out.at[:, pl.ds(256 * i, 256)], semaphores.at[i]
        )
        copy.start()
        copies.append(copy)
    for copy in copies:
        copy.wait()


def adam_rows(gradient, live_mask, first_moment, second_moment):
    new_first = jnp.where(live_mask, beta_one * first_moment + (1.0 - beta_one) * gradient, 0.0)
    new_second = jnp.where(
        live_mask, beta_two * second_moment + (1.0 - beta_two) * gradient * gradient, 0.0
    )
    first_hat = new_first / (1.0 - beta_one**STEP)
    second_hat = new_second / (1.0 - beta_two**STEP)
    update = jnp.where(live_mask, first_hat / (jnp.sqrt(second_hat) + adam_eps), 0.0)
    return (new_first, new_second, update.astype(BF16))


def per_device(
    activations, grad_output, projection, piece_lengths, piece_owners, first_moment, second_moment
):
    tokens = activations[0]
    grads = grad_output[0]
    y = lax.axis_index("fsdp").astype(jnp.int32) // 4
    slices = [lax.dynamic_slice(tokens, (0, (y + s) % 4 * 2048), (64, 2048)) for s in range(4)]
    *slices[1:], block, lengths = lax.optimization_barrier(
        (*slices[1:], projection, piece_lengths)
    )
    where = scalar_table(lengths, piece_owners)
    for s in (1, 3, 2):
        slices[s] = y_shift(slices[s], s)
    over_x = fsdp_flip(block, 2)
    over_core = fsdp_flip(block, 1)

    chosen = local_call(
        choose_kernel,
        "choose",
        [jax.ShapeDtypeStruct((512, 384), BF16)] * 2,
        (where, projection),
        2 * 512 * 512 * 768,
        scratch=[pltpu.VMEM((512, 512), BF16), pltpu.SemaphoreType.DMA],
        limit=8,
        anywhere=(1, 0),
    )
    over_x, where, *slices[1:] = lax.optimization_barrier((over_x, where, *slices[1:]))
    over_both = fsdp_flip(over_x, 1)
    (partial,) = local_call(
        front_kernel,
        "front",
        [jax.ShapeDtypeStruct((256, 512), F32)],
        (where, *slices, over_core, over_x, block),
        2 * 256 * 1536 * 512,
        scratch=[pltpu.VMEM((512, 512), BF16), pltpu.SemaphoreType.DMA],
        limit=8,
        anywhere=(1, 0),
    )
    mine, *partial = local_call(
        front_rest_kernel,
        "front_rest",
        [jax.ShapeDtypeStruct((64, 512), F32)] + [jax.ShapeDtypeStruct((64, 512), BF16)] * 3,
        (where, *slices, over_both, partial),
        2 * 256 * 512 * 512,
        limit=8,
    )
    same, cross, mine = lax.optimization_barrier((*chosen, mine))
    (projected,) = local_call(
        total_kernel,
        "total",
        [jax.ShapeDtypeStruct((64, 512), BF16)],
        (where, mine, *[y_shift(partial[s - 1], -s) for s in (1, 3, 2)]),
        64 * 512 * 4,
        limit=4,
    )

    (own,) = local_call(
        join_kernel,
        "join",
        [jax.ShapeDtypeStruct((512, 128), BF16)],
        (where, projected, tp_shift(projected, 0, 1)),
        64 * 512 * 4,
        limit=4,
    )
    up1, down1 = tp_shift(own, 1, 0), tp_shift(own, -1, 0)
    far = tp_shift(own, 4, 0)
    up2, down2 = tp_shift(up1, 1, 0), tp_shift(down1, -1, 0)
    table = [jax.ShapeDtypeStruct((512, FF), F32)]
    one = 2 * 512 * 128 * FF
    (gradient,) = local_call(
        functools.partial(sum_kernel, (0, 7, 1)),
        "near_terms",
        table,
        (where, own, up1, down1, grads),
        3 * one,
        cheap=True,
    )
    up2, down2, gradient = lax.optimization_barrier((up2, down2, gradient))
    up3, down3 = tp_shift(up2, 1, 0), tp_shift(down2, -1, 0)
    (gradient,) = local_call(
        functools.partial(sum_kernel, (6, 2)),
        "middle_terms",
        table,
        (where, up2, down2, grads, gradient),
        2 * one,
        aliases={4: 0},
        cheap=True,
    )
    give, rows = local_call(
        functools.partial(last_kernel, (5, 3, 4)),
        "last_terms",
        [jax.ShapeDtypeStruct((8, 48, FF), BF16), jax.ShapeDtypeStruct((560, FF), F32)],
        (where, up3, down3, far, grads, gradient),
        3 * one,
    )
    (keep,) = local_call(
        keep_kernel, "keep", [jax.ShapeDtypeStruct((8, 48, FF), F32)], (where, rows), 8 * 48 * FF
    )

    narrow, wide = jax.ShapeDtypeStruct((48, FF), BF16), jax.ShapeDtypeStruct((48, FF), F32)
    size = 48 * FF
    given = fsdp_flip(give, 1)
    up_x, down_x, far_x = local_call(
        functools.partial(pair_kernel, 0),
        "pair_first",
        [narrow] * 3,
        (where, keep, given),
        3 * size,
        limit=8,
    )
    up_x, down_x, far_x = y_shift(up_x, 1), y_shift(down_x, -1), fsdp_flip(far_x, 2)
    up, down, beside, far, mine = local_call(
        functools.partial(pair_kernel, 3),
        "pair_rest",
        [narrow] * 2 + [wide] * 3,
        (where, keep, given),
        5 * size,
        limit=8,
    )
    up, down = y_shift(up, 1), y_shift(down, -1)
    (far,) = local_call(add_kernel, "add_far", [narrow], (where, far, far_x), size, limit=8)
    far = y_shift(far, 2)
    (mine,) = local_call(
        add_kernel, "add_direct", [wide], (where, mine, up, down), 2 * size, limit=8
    )
    (beside,) = local_call(
        add_kernel, "add_beside", [narrow], (where, beside, up_x, down_x), 2 * size, limit=8
    )
    beside = fsdp_flip(beside, 2)
    update, gradient = local_call(
        update_kernel,
        "update",
        [narrow, wide],
        (where, mine, far, beside, first_moment, second_moment),
        30 * size,
        limit=8,
    )

    beside = fsdp_flip(update, 2)
    update, new_first = local_call(
        first_kernel,
        "first_moments",
        [narrow, wide],
        (where, update, gradient, first_moment),
        15 * size,
        limit=8,
    )
    (new_second,) = local_call(
        second_kernel, "second_moments", [wide], (where, gradient, second_moment), 15 * size, limit=8
    )
    up, down, far = y_shift(update, 1), y_shift(update, -1), y_shift(update, 2)
    up_x, down_x, far_x = y_shift(beside, 1), y_shift(beside, -1), fsdp_flip(far, 2)
    updates = jnp.concatenate([update, beside, up, down, far, up_x, down_x, far_x], axis=0)
    crossed = fsdp_flip(updates, 1)
    (delta,) = local_call(
        half_delta_kernel, "half_delta", table, (where, same, updates), 2 * 512 * 384 * FF
    )
    (weight_delta,) = local_call(
        delta_kernel,
        "delta",
        [jax.ShapeDtypeStruct((512, FF), BF16)],
        (where, cross, crossed, delta),
        2 * 512 * 384 * FF,
        scratch=[pltpu.VMEM((512, FF), BF16), pltpu.SemaphoreType.DMA((7,))],
        anywhere=(0, 1),
    )
    return (weight_delta, new_first, new_second)


def solution(mesh):
    return jax.shard_map(
        per_device,
        mesh=mesh,
        in_specs=(
            P("fsdp", "tp", None),
            P("fsdp", None, "tp"),
            P("fsdp", None),
            P(),
            P(),
            P("fsdp", "tp"),
            P("fsdp", "tp"),
        ),
        out_specs=(P("fsdp", "tp"), P("fsdp", "tp"), P("fsdp", "tp")),
        check_vma=False,
    )
```

```python
import functools

import jax
import jax.numpy as jnp
from jax import lax
from jax.experimental import pallas as pl
from jax.experimental.pallas import tpu as pltpu
from jax.sharding import PartitionSpec as P

STEP = 10
beta_one = 0.9
beta_two = 0.999
adam_eps = 1e-08

F32 = jnp.float32
BF16 = jnp.bfloat16

LOW, Z, CORE, H, Y, X, F, START, LENGTH = 0, 1, 2, 3, 4, 5, 6, 16, 32
TO_CHIPS = [(1, 1), (3, 1), (2, 1), (1, 0), (3, 0), (0, 1), (2, 0), (0, 0)]
FROM_CHIPS = [(0, 0), (0, 1), (3, 0), (1, 0), (2, 0), (3, 1), (1, 1), (2, 1)]
FF = 1792
VMEM = pltpu.VMEM


def fsdp_flip(value, flip):
    return lax.ppermute(value, "fsdp", [(i, i ^ flip) for i in range(16)])


def y_shift(value, dy):
    return lax.ppermute(value, "fsdp", [(i, (i + 4 * dy) % 16) for i in range(16)])


def tp_shift(value, dz, dh):
    pairs = [(i, ((i // 2 + dz) % 8) * 2 + ((i % 2) ^ dh)) for i in range(16)]
    return lax.ppermute(value, "tp", pairs)


SCALARS = pl.BlockSpec(memory_space=pltpu.SMEM)
ANYWHERE = pl.BlockSpec(memory_space=pl.ANY)


def in_vmem(count):
    return [pl.BlockSpec(memory_space=VMEM)] * count


def local_call(
    kernel, name, out_shape, operands, flops, scratch=(), limit=24, aliases=None, anywhere=(0, 0), cheap=False
):
    size = sum(v.size * v.dtype.itemsize for v in operands)
    if cheap:
        flops, size = 1 << 10, 1 << 10
    return pl.pallas_call(
        kernel,
        in_specs=[SCALARS] + in_vmem(len(operands) - 1 - anywhere[0]) + [ANYWHERE] * anywhere[0],
        out_specs=in_vmem(len(out_shape) - anywhere[1]) + [ANYWHERE] * anywhere[1],
        out_shape=out_shape,
        scratch_shapes=scratch,
        input_output_aliases=aliases or {},
        cost_estimate=pl.CostEstimate(flops=flops, bytes_accessed=size, transcendentals=0),
        compiler_params=pltpu.CompilerParams(vmem_limit_bytes=limit << 20),
        name=name,
    )(*operands)


def table_kernel(lengths, owners, out):
    f = lax.axis_index("fsdp").astype(jnp.int32)
    c = lax.axis_index("tp").astype(jnp.int32)
    facts = {LOW: f % 4, Z: c // 2, CORE: f % 2, H: c % 2, Y: f // 4, X: f // 2 % 2, F: f}
    for place, value in facts.items():
        out[place] = value
    start = jnp.int32(0)
    for piece in range(16):
        owner = owners[piece]
        out[START + owner] = start
        out[LENGTH + owner] = lengths[piece]
        start = start + lengths[piece]


def scalar_table(lengths, owners):
    return pl.pallas_call(
        table_kernel,
        in_specs=[SCALARS] * 2,
        out_specs=SCALARS,
        out_shape=jax.ShapeDtypeStruct((48,), jnp.int32),
        cost_estimate=pl.CostEstimate(flops=0, bytes_accessed=512, transcendentals=0),
        compiler_params=pltpu.CompilerParams(vmem_limit_bytes=1 << 20),
        name="table",
    )(lengths, owners)


def owner_of(where, dy, dx, other):
    chip = lax.rem(where[Y] + dy, 4) * 2 + (where[X] ^ dx)
    return chip * 2 + (where[CORE] ^ other)


def choose_kernel(where, source, *refs):
    *outs, projection, semaphore = refs
    copy = pltpu.make_async_copy(source, projection, semaphore)
    copy.start()
    row = lax.broadcasted_iota(jnp.int32, (48, 512), 1)
    slot = lax.broadcasted_iota(jnp.int32, (48, 512), 0)
    for other, out in enumerate(outs):
        marks = []
        for dy, dx in FROM_CHIPS:
            owner = owner_of(where, dy, dx, other)
            live = (row == where[START + owner] + slot) & (slot < where[LENGTH + owner])
            marks.append(jnp.where(live, 1.0, 0.0))
        hot = jnp.concatenate(marks, axis=0).astype(BF16)
        if other == 0:
            copy.wait()
        out[...] = lax.dot_general(
            projection[...], hot, (((1,), (1,)), ((), ())), preferred_element_type=F32
        ).astype(BF16)


def token_product(where, r, tokens, block):
    columns = pl.ds(pl.multiple_of((where[LOW] ^ r) * 512, 512), 512)
    rows = jnp.concatenate([t[:, columns] for t in tokens], axis=0)
    return jnp.dot(rows, block[...], preferred_element_type=F32)


def front_kernel(where, a0, a1, a2, a3, p1, p2, p0, out, here, semaphore):
    copy = pltpu.make_async_copy(p0, here, semaphore)
    copy.start()
    tokens = (a0, a1, a2, a3)
    total = token_product(where, 1, tokens, p1) + token_product(where, 2, tokens, p2)
    copy.wait()
    out[...] = total + token_product(where, 0, tokens, here)


def front_rest_kernel(where, a0, a1, a2, a3, p3, before, o0, o1, o2, o3):
    total = before[...] + token_product(where, 3, (a0, a1, a2, a3), p3)
    for i, o in enumerate((o0, o1, o2, o3)):
        o[...] = total[i * 64 : (i + 1) * 64].astype(o.dtype)


def total_kernel(_, a, b, c, d, out):
    others = b[...].astype(F32) + c[...].astype(F32) + d[...].astype(F32)
    out[...] = (a[...] + others).astype(BF16)


def join_kernel(where, mine, partner, out):
    first = where[H] == 0
    here, there = mine[...].astype(F32), partner[...].astype(F32)
    rows = jnp.concatenate(
        [jnp.where(first, here, there), jnp.where(first, there, here)], axis=0
    )
    out[...] = rows.T.astype(BF16)


def token_rows(where, grads, offset):
    row = lax.rem(where[Z] + offset, 8) * 128
    return grads[pl.ds(pl.multiple_of(row, 128), 128), :]


def sum_kernel(offsets, where, *refs):
    count = len(offsets)
    blocks, grads, rest, out = refs[:count], refs[count], refs[count + 1 : -1], refs[-1]
    left = jnp.concatenate([b[...] for b in blocks], axis=1)
    right = jnp.concatenate([token_rows(where, grads, o) for o in offsets], axis=0)
    total = jnp.dot(left, right, preferred_element_type=F32)
    for before in rest:
        total = total + before[...]
    out[...] = total


def rows_from(table, start):
    low = lax.rem(start, 8)
    rows = table[pl.ds(pl.multiple_of(start - low, 8), 56), :]
    return pltpu.roll(rows, lax.rem(56 - low, 56), 0)[:48]


def last_kernel(offsets, where, *refs):
    give, table = refs[-2:]
    table[512:560, :] = jnp.zeros((48, FF), F32)
    sum_kernel(offsets, where, *refs[:-2], table.at[0:512, :])
    for i, (dy, dx) in enumerate(TO_CHIPS):
        give[i] = rows_from(table, where[START + owner_of(where, dy, dx, 1)]).astype(BF16)


def keep_kernel(where, table, keep):
    for i, (dy, dx) in enumerate(TO_CHIPS):
        keep[i] = rows_from(table, where[START + owner_of(where, dy, dx, 0)])


def pair_kernel(first, _, keep, given, *outs):
    for i, out in enumerate(outs, first):
        out[...] = (keep[i] + given[i].astype(F32)).astype(out.dtype)


def add_kernel(_, *refs):
    total = refs[0][...]
    for r in refs[1:-1]:
        total = total + r[...].astype(F32)
    refs[-1][...] = total.astype(refs[-1].dtype)


def update_kernel(where, own, t1, t2, first, second, update, gradient):
    live = lax.broadcasted_iota(jnp.int32, (48, FF), 0) < where[LENGTH + where[F]]
    total = own[...]
    for t in (t1, t2):
        total = total + t[...].astype(F32)
    gradient[...] = total
    update[...] = adam_rows(total, live, first[...], second[...])[2]


def first_kernel(where, update, gradient, first, again, new_first):
    live = lax.broadcasted_iota(jnp.int32, (48, FF), 0) < where[LENGTH + where[F]]
    again[...] = update[...]
    new_first[...] = adam_rows(gradient[...], live, first[...], jnp.zeros((48, FF), F32))[0]


def second_kernel(where, gradient, second, new_second):
    live = lax.broadcasted_iota(jnp.int32, (48, FF), 0) < where[LENGTH + where[F]]
    new_second[...] = adam_rows(gradient[...], live, jnp.zeros((48, FF), F32), second[...])[1]


def half_delta_kernel(_, chosen, updates, out):
    out[...] = jnp.dot(chosen[...], updates[...], preferred_element_type=F32)


def delta_kernel(_, chosen, updates, before, out, whole, semaphores):
    copies = []
    for i in range(7):
        columns = slice(256 * i, 256 * i + 256)
        product = jnp.dot(chosen[...], updates[:, columns], preferred_element_type=F32)
        whole[:, columns] = (before[:, columns] + product).astype(BF16)
        copy = pltpu.make_async_copy(
            whole.at[:, pl.ds(256 * i, 256)], out.at[:, pl.ds(256 * i, 256)], semaphores.at[i]
        )
        copy.start()
        copies.append(copy)
    for copy in copies:
        copy.wait()


def adam_rows(gradient, live_mask, first_moment, second_moment):
    new_first = jnp.where(live_mask, beta_one * first_moment + (1.0 - beta_one) * gradient, 0.0)
    new_second = jnp.where(
        live_mask, beta_two * second_moment + (1.0 - beta_two) * gradient * gradient, 0.0
    )
    first_hat = new_first / (1.0 - beta_one**STEP)
    second_hat = new_second / (1.0 - beta_two**STEP)
    update = jnp.where(live_mask, first_hat / (jnp.sqrt(second_hat) + adam_eps), 0.0)
    return (new_first, new_second, update.astype(BF16))


def per_device(
    activations, grad_output, projection, piece_lengths, piece_owners, first_moment, second_moment
):
    tokens = activations[0]
    grads = grad_output[0]
    y = lax.axis_index("fsdp").astype(jnp.int32) // 4
    def token_slice(source, s):
        return lax.dynamic_slice(source, (0, (y + s) % 4 * 2048), (64, 2048))

    *slices, rest, block, lengths = lax.optimization_barrier(
        (*[token_slice(tokens, s) for s in (1, 2, 3)], tokens, projection, piece_lengths)
    )
    slices = [token_slice(rest, 0), *slices]
    where = scalar_table(lengths, piece_owners)
    for s in (1, 3, 2):
        slices[s] = y_shift(slices[s], s)
    over_x = fsdp_flip(block, 2)
    over_core = fsdp_flip(block, 1)

    chosen = local_call(
        choose_kernel,
        "choose",
        [jax.ShapeDtypeStruct((512, 384), BF16)] * 2,
        (where, projection),
        2 * 512 * 512 * 768,
        scratch=[pltpu.VMEM((512, 512), BF16), pltpu.SemaphoreType.DMA],
        limit=8,
        anywhere=(1, 0),
    )
    over_x, where, *slices[1:] = lax.optimization_barrier((over_x, where, *slices[1:]))
    over_both = fsdp_flip(over_x, 1)
    (partial,) = local_call(
        front_kernel,
        "front",
        [jax.ShapeDtypeStruct((256, 512), F32)],
        (where, *slices, over_core, over_x, block),
        2 * 256 * 1536 * 512,
        scratch=[pltpu.VMEM((512, 512), BF16), pltpu.SemaphoreType.DMA],
        limit=8,
        anywhere=(1, 0),
    )
    mine, *partial = local_call(
        front_rest_kernel,
        "front_rest",
        [jax.ShapeDtypeStruct((64, 512), F32)] + [jax.ShapeDtypeStruct((64, 512), BF16)] * 3,
        (where, *slices, over_both, partial),
        2 * 256 * 512 * 512,
        limit=8,
    )
    same, cross, mine = lax.optimization_barrier((*chosen, mine))
    (projected,) = local_call(
        total_kernel,
        "total",
        [jax.ShapeDtypeStruct((64, 512), BF16)],
        (where, mine, *[y_shift(partial[s - 1], -s) for s in (1, 3, 2)]),
        64 * 512 * 4,
        limit=4,
    )

    (own,) = local_call(
        join_kernel,
        "join",
        [jax.ShapeDtypeStruct((512, 128), BF16)],
        (where, projected, tp_shift(projected, 0, 1)),
        64 * 512 * 4,
        limit=4,
    )
    up1, down1 = tp_shift(own, 1, 0), tp_shift(own, -1, 0)
    far = tp_shift(own, 4, 0)
    up2, down2 = tp_shift(up1, 1, 0), tp_shift(down1, -1, 0)
    table = [jax.ShapeDtypeStruct((512, FF), F32)]
    one = 2 * 512 * 128 * FF
    (gradient,) = local_call(
        functools.partial(sum_kernel, (0, 7, 1)),
        "near_terms",
        table,
        (where, own, up1, down1, grads),
        3 * one,
        cheap=True,
    )
    up2, down2, gradient = lax.optimization_barrier((up2, down2, gradient))
    up3, down3 = tp_shift(up2, 1, 0), tp_shift(down2, -1, 0)
    (gradient,) = local_call(
        functools.partial(sum_kernel, (6, 2)),
        "middle_terms",
        table,
        (where, up2, down2, grads, gradient),
        2 * one,
        aliases={4: 0},
        cheap=True,
    )
    give, rows = local_call(
        functools.partial(last_kernel, (5, 3, 4)),
        "last_terms",
        [jax.ShapeDtypeStruct((8, 48, FF), BF16), jax.ShapeDtypeStruct((560, FF), F32)],
        (where, up3, down3, far, grads, gradient),
        3 * one,
    )
    (keep,) = local_call(
        keep_kernel, "keep", [jax.ShapeDtypeStruct((8, 48, FF), F32)], (where, rows), 8 * 48 * FF
    )

    narrow, wide = jax.ShapeDtypeStruct((48, FF), BF16), jax.ShapeDtypeStruct((48, FF), F32)
    size = 48 * FF
    given = fsdp_flip(give, 1)
    up_x, down_x, far_x = local_call(
        functools.partial(pair_kernel, 0),
        "pair_first",
        [narrow] * 3,
        (where, keep, given),
        3 * size,
        limit=8,
    )
    up_x, down_x, far_x = y_shift(up_x, 1), y_shift(down_x, -1), fsdp_flip(far_x, 2)
    up, down, beside, far, mine = local_call(
        functools.partial(pair_kernel, 3),
        "pair_rest",
        [narrow] * 2 + [wide] * 3,
        (where, keep, given),
        5 * size,
        limit=8,
    )
    up, down = y_shift(up, 1), y_shift(down, -1)
    (far,) = local_call(add_kernel, "add_far", [narrow], (where, far, far_x), size, limit=8)
    far = y_shift(far, 2)
    (mine,) = local_call(
        add_kernel, "add_direct", [wide], (where, mine, up, down), 2 * size, limit=8
    )
    (beside,) = local_call(
        add_kernel, "add_beside", [narrow], (where, beside, up_x, down_x), 2 * size, limit=8
    )
    beside = fsdp_flip(beside, 2)
    update, gradient = local_call(
        update_kernel,
        "update",
        [narrow, wide],
        (where, mine, far, beside, first_moment, second_moment),
        30 * size,
        limit=8,
    )

    beside = fsdp_flip(update, 2)
    update, new_first = local_call(
        first_kernel,
        "first_moments",
        [narrow, wide],
        (where, update, gradient, first_moment),
        15 * size,
        limit=8,
    )
    (new_second,) = local_call(
        second_kernel, "second_moments", [wide], (where, gradient, second_moment), 15 * size, limit=8
    )
    up, down, far = y_shift(update, 1), y_shift(update, -1), y_shift(update, 2)
    up_x, down_x, far_x = y_shift(beside, 1), y_shift(beside, -1), fsdp_flip(far, 2)
    updates = jnp.concatenate([update, beside, up, down, far, up_x, down_x, far_x], axis=0)
    crossed = fsdp_flip(updates, 1)
    (delta,) = local_call(
        half_delta_kernel, "half_delta", table, (where, same, updates), 2 * 512 * 384 * FF
    )
    (weight_delta,) = local_call(
        delta_kernel,
        "delta",
        [jax.ShapeDtypeStruct((512, FF), BF16)],
        (where, cross, crossed, delta),
        2 * 512 * 384 * FF,
        scratch=[pltpu.VMEM((512, FF), BF16), pltpu.SemaphoreType.DMA((7,))],
        anywhere=(0, 1),
    )
    return (weight_delta, new_first, new_second)


def solution(mesh):
    return jax.shard_map(
        per_device,
        mesh=mesh,
        in_specs=(
            P("fsdp", "tp", None),
            P("fsdp", None, "tp"),
            P("fsdp", None),
            P(),
            P(),
            P("fsdp", "tp"),
            P("fsdp", "tp"),
        ),
        out_specs=(P("fsdp", "tp"), P("fsdp", "tp"), P("fsdp", "tp")),
        check_vma=False,
    )
```
